32 devices in a mesh: grp: 2 (over y), gx: 4 (over z), gy: 2 (over x), gz: 2 (over core).
Axes of the slice: x: 2, y: 2, z: 4, core: 2. Of those that a mesh axis runs over, the one named last changes fastest.
Arguments:
- parcel_values: bfloat16 [6, 131072], P(None, ('grp', 'gx', 'gy', 'gz')), parts along dimension 1, may hold values from -2304 to 2304
- parcel_owner: int32 [131072, 1], P(('grp', 'gx', 'gy', 'gz')), parts along dimension 0, may hold values from 0 to 3; in each aligned block of 4096 rows (0 to 4095, 4096 to 8191, ...) at most 1536 rows name the same one
- parcel_cell: int32 [131072], P(('grp', 'gx', 'gy', 'gz')), parts along dimension 0, may hold values from 0 to 65535
- live_counts: int32 [32], P(('grp', 'gx', 'gy', 'gz')), parts along dimension 0, may hold values from 1 to 4096, 49152 in all
- fluid_state: bfloat16 [6, 256, 32, 256], P(None, ('grp', 'gx'), 'gy', 'gz'), parts along dimension 1, may hold values from -6 to 6
Outputs:
- coupled: bfloat16 [6, 256, 32, 256], P(None, ('grp', 'gx'), 'gy', 'gz'), parts along dimension 1
The draws below stay inside these ranges and needn't reach their ends.
There are 2 independent parts, one for each index of `grp`. The reference program is written for one: setup_inputs(seed, part) draws one part's arguments, and reference() takes and returns one part's arrays. A program takes and returns all parts, laid end to end along the dimension named above; each array names one. Nothing has to cross between parts.
Inputs may be any that keep to these rules, and one draw needn't show every extreme that they name: `parcel_owner`: among the rows of one brick no streamwise index is named by more than 1536 rows; some brick names one exactly 1536 times. `parcel_cell`: cells are numbered (x * 16 + y) * 128 + z within the brick. `live_counts`: A brick's live parcels are its first rows; some brick has all rows live.
All inputs are finite; a program needn't handle non-finite values. No bound on the sum of `live_counts` on one device may be relied on, other than what follows from the above.
Results may differ from the reference program's by a relative error of at most 0.005.
Values may be sent and summed in bfloat16 or wider, within the bound.
A program may use at most 64 MiB of HBM per device.

```python
import math
import jax
import jax.numpy as jnp
import numpy as np
from jax import lax

CH = 6
REACH = 16
BX = 32
BY = 16
BZ = 128
P_DEV = 4096
CAP = 1536
BRICKS = 16
PARCELS = 65536
CELLS = 65536
NX = 128
NY = 32
NZ = 256
N_GX = 4
N_GY = 2
N_GZ = 2


def touch_ends(values, key, least, top_value):
    longest = values.shape.index(max(values.shape))
    spots = []
    for shift in (0, 1):
        where = [jax.random.randint(jax.random.fold_in(key, axis), (), 0, length) for axis, length in enumerate(values.shape)]
        where[longest] = (where[longest] + shift) % values.shape[longest]
        spots.append(tuple(where))
    return values.at[spots[0]].set(least).at[spots[1]].set(top_value)


def levels(rng, dims, shards, low, top_value):
    level, own = 1.0, jax.random.fold_in(rng, 6)
    for axis_at, blocks in shards:
        steps = jnp.exp(jax.random.uniform(jax.random.fold_in(own, axis_at), (blocks,), jnp.float32, low / len(shards), top_value / len(shards)))
        level = level * jnp.repeat(steps, dims[axis_at] // blocks).reshape([-1 if axis == axis_at else 1 for axis in range(len(dims))])
    return level


def length_profile(count, total, bound, slope):
    loads = [(1 << 20) // math.isqrt(grade ** slope) + 1 for grade in range(2, count + 1)]
    spare, given = total - bound - (count - 1), [1] * (count - 1)
    while spare > 0:
        movable = [i for i in range(count - 1) if given[i] < bound]
        whole, budget = sum([loads[i] for i in movable]), spare
        for i in movable:
            addition = min(bound - given[i], max(1, budget * loads[i] // whole), spare)
            given[i] = given[i] + addition
            spare = spare - addition
    return np.array([bound] + given)


def uneven_parts(key, count, total, limit, skew):
    if count == 2:
        one = jax.random.randint(key, (), max(1, total - limit), min(limit, total - 1) + 1)
        return jnp.stack([one, total - one])
    sizes = jnp.asarray(length_profile(count, total, limit, skew), jnp.int32)
    twos = (count - 1) // 2
    source_of, receiver = sizes[1:1 + 2 * twos:2], sizes[2:2 + 2 * twos:2]
    margin = jnp.minimum(source_of - 1, limit - receiver)
    shifted = jax.random.randint(jax.random.fold_in(key, 1), (twos,), 0, 1 << 20) % (margin + 1)
    sizes = sizes.at[1:1 + 2 * twos:2].set(source_of - shifted).at[2:2 + 2 * twos:2].set(receiver + shifted)
    return sizes[jax.random.permutation(jax.random.fold_in(key, 2), count)]


def deal_out(own_key, own, number, rows, amount, top, reach, lean):
    ranking = jax.random.permutation(own_key, amount)
    crowded, common = load_shares(amount, rows * top, reach, lean, True), load_shares(amount, rows * top, reach, lean, False)
    places = jnp.arange(amount)

    def named(tallies, offset_by):
        used = int((tallies > 0).sum())
        fixed = max(1, used // 4)
        moved = fixed + (places - fixed + offset_by * (used - fixed)) % max(1, amount - fixed)
        return jnp.zeros((amount,), jnp.int32).at[ranking[jnp.where(places < fixed, places, moved)]].set(jnp.asarray(tallies, jnp.int32))

    tallies = jnp.where(number % 4 == 0, named(crowded, number // 4), named(common, number - number // 4 - 1))
    mixed = jax.random.permutation(jax.random.fold_in(own, 3), amount)
    giver, sink = mixed[0:amount // 2 * 2:2], mixed[1:amount // 2 * 2:2]
    room = jnp.minimum(tallies[giver] - 1, reach - tallies[sink]) // 2
    room = jnp.where((giver == ranking[0]) | (sink == ranking[0]) | (tallies[sink] == 0), 0, jnp.maximum(room, 0))
    moved = jax.random.randint(jax.random.fold_in(own, 4), (amount // 2,), 0, 1 << 20) % (room + 1)
    tallies = tallies.at[giver].add(-moved).at[sink].add(moved)
    labels = jnp.searchsorted(jnp.cumsum(tallies), jnp.arange(rows * top), side="right").astype(jnp.int32)
    listing = labels.reshape(top, rows).T
    listing = listing[jax.random.permutation(jax.random.fold_in(own, 1), rows)]
    offset_by = jax.random.randint(jax.random.fold_in(own, 2), (rows, 1), 0, top)
    return jnp.take_along_axis(listing, (jnp.arange(top)[None, :] + offset_by) % top, axis=1)


def load_shares(amount, total, reach, lean, full):
    weights = [(1 << 20) // math.isqrt(grade ** lean) + 1 for grade in range(1, amount + 1)]
    largest = reach if full else min(reach, max(-(-total // amount), total * weights[0] // sum(weights)))
    least = 1 if total - largest >= amount - 1 else 0
    counts, rest = [largest] + [least] * (amount - 1), total - largest - least * (amount - 1)
    while rest > 0:
        free = [i for i in range(1, amount) if counts[i] < largest] or [i for i in range(1, amount) if counts[i] < reach]
        pool, remaining = sum([weights[i] for i in free]), rest
        for i in free:
            extra = min(reach - counts[i], max(1, remaining * weights[i] // pool), rest)
            counts[i] = counts[i] + extra
            rest = rest - extra
    return np.array(counts)


def bell_draw(rng, extent, width, limit, pieces=(), kind=jnp.bfloat16):
    gain = levels(rng, extent, pieces, -0.22, 0.18) if pieces else 1.0
    values = jax.random.normal(rng, extent, jnp.float32) * width * gain
    return jnp.minimum(jnp.maximum(values, -limit), limit).astype(kind)


def setup_inputs(seed: int = 0, part: int = 0) -> dict:
    keys = jax.random.split(jax.random.key(seed), 6)
    part_keys = jax.random.split(jax.random.fold_in(keys[5], part), 6)
    parcel_values = bell_draw(part_keys[0], (CH, PARCELS), 384.0, 2304.0, ((1, 16),))
    parcel_owner_keys = jax.random.split(jax.random.fold_in(part_keys[1], 1), PARCELS // P_DEV)
    parcel_owner_turns = jax.random.permutation(jax.random.fold_in(part_keys[1], 3), PARCELS // P_DEV)
    parcel_owner = jax.vmap(lambda own, number: deal_out(jax.random.fold_in(part_keys[1], 2), own, number, P_DEV, N_GX, 1, CAP, 2))(parcel_owner_keys, parcel_owner_turns).reshape((PARCELS, 1))
    parcel_cell = touch_ends(jax.random.randint(part_keys[2], (PARCELS,), 0, CELLS), jax.random.fold_in(part_keys[2], 1), 0, CELLS - 1).astype(jnp.int32)
    live_counts = uneven_parts(part_keys[3], BRICKS, 3 * P_DEV * BRICKS // 4, P_DEV, 2).astype(jnp.int32)
    fluid_state = bell_draw(part_keys[4], (CH, NX, NY, NZ), 1.0, 6.0, ((1, 4), (2, 2), (3, 2)))
    return dict(parcel_values=parcel_values, parcel_owner=parcel_owner, parcel_cell=parcel_cell, live_counts=live_counts, fluid_state=fluid_state)


spread_cells = 12.0


def tap_curve(offsets):
    tap_grid = jnp.arange(2 * REACH + 1).astype(jnp.float32)
    tap_sum = jnp.sum(jnp.exp(-(tap_grid - REACH) * (tap_grid - REACH) / (2.0 * spread_cells * spread_cells)))
    return jnp.exp(-(offsets - REACH) * (offsets - REACH) / (2.0 * spread_cells * spread_cells)) / tap_sum


def reference(parcel_values, parcel_owner, parcel_cell, live_counts, fluid_state):
    parcels = parcel_values.shape[1]
    row_ids = jnp.arange(parcels, dtype=jnp.int32)
    brick_id = row_ids // P_DEV
    is_live = (row_ids % P_DEV) < live_counts[brick_id]
    brick_y = (brick_id // N_GZ) % N_GY
    brick_z = brick_id % N_GZ
    pos_x = parcel_owner[:, 0] * BX + parcel_cell // (BY * BZ)
    pos_y = brick_y * BY + (parcel_cell // BZ) % BY
    pos_z = brick_z * BZ + parcel_cell % BZ
    weights = jnp.where(is_live[None, :], parcel_values.astype(jnp.float32), 0.0)
    source = jnp.zeros((CH, NX, NY, NZ), jnp.float32).at[:, pos_x, pos_y, pos_z].add(weights)
    source = lax.optimization_barrier(source.astype(jnp.bfloat16)).astype(jnp.float32)
    taps = tap_curve(jnp.arange(2 * REACH + 1).astype(jnp.float32))
    taps = lax.optimization_barrier(taps.astype(jnp.bfloat16)).astype(jnp.float32)
    padded = jnp.pad(source, ((0, 0), (REACH, REACH), (0, 0), (0, 0)))
    after_x = jnp.zeros((CH, NX, NY, NZ), jnp.float32)
    for offset in range(2 * REACH + 1):
        after_x = after_x + taps[offset] * padded[:, offset:offset + NX]
    after_x = lax.optimization_barrier(after_x.astype(jnp.bfloat16)).astype(jnp.float32)
    after_y = jnp.zeros((CH, NX, NY, NZ), jnp.float32)
    for offset in range(2 * REACH + 1):
        after_y = after_y + taps[offset] * jnp.roll(after_x, REACH - offset, axis=2)
    after_y = lax.optimization_barrier(after_y.astype(jnp.bfloat16)).astype(jnp.float32)
    summed = fluid_state.astype(jnp.float32)
    for offset in range(2 * REACH + 1):
        summed = summed + taps[offset] * jnp.roll(after_y, REACH - offset, axis=3)
    return summed.astype(jnp.bfloat16)
```

```python
import functools
import math

import jax
import jax.numpy as jnp
import numpy as np
from jax import lax
from jax.experimental import pallas as pl
from jax.experimental.pallas import tpu as pltpu
from jax.sharding import PartitionSpec as P

REACH = 16


spread_cells = 12.0


def padded(shard, sides, width):
    for axis, dim in sides:
        size, length = (lax.axis_size(axis), shard.shape[dim])
        up = [(i, (i + 1) % size) for i in range(size)]
        down = [(j, i) for i, j in up]
        last = lax.slice_in_dim(shard, length - width, length, axis=dim)
        initial = lax.slice_in_dim(shard, 0, width, axis=dim)
        before = lax.ppermute(last, axis, up)
        after = lax.ppermute(initial, axis, down)
        shard = jnp.concatenate([before, shard, after], axis=dim)
    return shard


def tap_curve(offsets):
    tap_grid = jnp.arange(2 * REACH + 1).astype(jnp.float32)
    tap_sum = jnp.sum(
        jnp.exp(-(tap_grid - REACH) * (tap_grid - REACH) / (2.0 * spread_cells * spread_cells))
    )
    return (
        jnp.exp(-(offsets - REACH) * (offsets - REACH) / (2.0 * spread_cells * spread_cells))
        / tap_sum
    )


def banded(out_rows, in_rows, shift):
    row_ids = lax.broadcasted_iota(jnp.int32, (out_rows, in_rows), 0)
    col_ids = lax.broadcasted_iota(jnp.int32, (out_rows, in_rows), 1)
    offset_ids = col_ids - row_ids + shift
    inside = (offset_ids >= 0) & (offset_ids <= 2 * REACH)
    values = tap_curve(offset_ids.astype(jnp.float32)).astype(jnp.bfloat16)
    return jnp.where(inside, values, jnp.zeros_like(values))


def running_sum(hits):
    shift = 1
    while shift < hits.shape[0]:
        hits = hits + jnp.pad(hits[:-shift], ((shift, 0), (0, 0)))
        shift *= 2
    return hits


def general(parcel_values, parcel_owner, parcel_cell, live_counts, fluid_state):
    channels, count_dev = parcel_values.shape
    width_x, width_y, width_z = (fluid_state.shape[1], fluid_state.shape[2], fluid_state.shape[3])
    owners = lax.axis_size("gx")
    capacity = 3 * count_dev // (2 * owners)
    owner_ids = parcel_owner[:, 0]
    local_rows = jnp.arange(count_dev, dtype=jnp.int32)
    is_live = local_rows < live_counts[0]
    owner_hits = (
        (owner_ids[:, None] == jnp.arange(owners, dtype=jnp.int32)[None, :]) & is_live[:, None]
    ).astype(jnp.int32)
    position = jnp.sum(running_sum(owner_hits) * owner_hits, axis=1) - 1
    slot_index = jnp.where(is_live, owner_ids * capacity + position, owners * capacity)
    cell_xpart = (parcel_cell // (width_y * width_z)).astype(jnp.bfloat16)
    cell_ypart = (parcel_cell // width_z % width_y).astype(jnp.bfloat16)
    cell_low = (parcel_cell % width_z).astype(jnp.bfloat16)
    send_rows = jnp.concatenate(
        [parcel_values, cell_xpart[None, :], cell_ypart[None, :], cell_low[None, :]], axis=0
    )
    packed = (
        jnp.zeros((channels + 3, owners * capacity), jnp.bfloat16)
        .at[:, slot_index]
        .set(send_rows, mode="drop")
    )
    packed = packed.reshape(channels + 3, owners, capacity)
    arrived = lax.all_to_all(packed, "gx", split_axis=1, concat_axis=1, tiled=True).reshape(
        channels + 3, owners * capacity
    )
    slot_total = owners * capacity
    block_rows = min(1024, slot_total)
    plane_cells = width_x * width_y
    high_grid = jnp.arange(plane_cells, dtype=jnp.float32)
    low_grid = jnp.arange(width_z, dtype=jnp.float32)

    def deposit(step_index, summed):
        window = lax.dynamic_slice_in_dim(arrived, step_index * block_rows, block_rows, 1)
        high_ids = window[channels].astype(jnp.float32) * width_y + window[channels + 1].astype(
            jnp.float32
        )
        high_hot = (high_ids[:, None] == high_grid[None, :]).astype(jnp.bfloat16)
        low_hot = (window[channels + 2].astype(jnp.float32)[:, None] == low_grid[None, :]).astype(
            jnp.bfloat16
        )
        weighted = window[:channels][:, :, None] * low_hot[None, :, :]
        return summed + jnp.einsum(
            "sh,csz->chz", high_hot, weighted, preferred_element_type=jnp.float32
        )

    summed = lax.fori_loop(
        0,
        slot_total // block_rows,
        deposit,
        jnp.zeros((channels, plane_cells, width_z), jnp.float32),
    )
    source = summed.reshape(channels, width_x, width_y, width_z).astype(jnp.bfloat16)
    flat_source = source.reshape(channels, width_x, width_y * width_z)
    pencil = lax.all_to_all(flat_source, "gx", split_axis=2, concat_axis=1, tiled=True)
    full_x = pencil.shape[1]
    smoothed = jnp.einsum(
        "ij,cjk->cik", banded(full_x, full_x, REACH), pencil, preferred_element_type=jnp.float32
    ).astype(jnp.bfloat16)
    after_x = lax.all_to_all(smoothed, "gx", split_axis=1, concat_axis=2, tiled=True)
    after_x = after_x.reshape(channels, width_x, width_y, width_z)
    extended_y = padded(after_x, (("gy", 2),), REACH)
    after_y = jnp.einsum(
        "ij,cxjz->cxiz",
        banded(width_y, width_y + 2 * REACH, 0),
        extended_y,
        preferred_element_type=jnp.float32,
    ).astype(jnp.bfloat16)
    extended_z = padded(after_y, (("gz", 3),), REACH)
    smooth_z = jnp.einsum(
        "cxyj,ij->cxyi",
        extended_z,
        banded(width_z, width_z + 2 * REACH, 0),
        preferred_element_type=jnp.float32,
    )
    return (fluid_state.astype(jnp.float32) + smooth_z).astype(jnp.bfloat16)


SEG = 256
STEP = 4
FIELDS = 3
PAIR = 2
FAR = 1024.0
TAP_SUM = float(
    sum(math.exp(-((t - REACH) ** 2) / (2.0 * spread_cells**2)) for t in range(2 * REACH + 1))
)


def tap_matrix(offsets):
    values = np.exp(-((offsets - REACH) ** 2) / (2.0 * spread_cells**2)) / TAP_SUM
    values = values.astype(np.float32).astype(jnp.bfloat16).astype(np.float32)
    return np.where((offsets >= 0) & (offsets <= 2 * REACH), values, 0.0)


def periodic_pair(width):
    out_at, in_at = np.arange(width)[:, None], np.arange(width)[None, :]
    own = tap_matrix(in_at - out_at + REACH)
    other = tap_matrix(in_at - width - out_at + REACH) + tap_matrix(in_at + width - out_at + REACH)
    return own, other


def fused(sizes, pay_ref, fluid_ref, wy_ref, wz_ref, out_ref, arrived, fields, weights, total,
          x_buf, x_in, z_buf, z_in, pay_send, pay_recv, zs_send, zs_recv, ys_send, ys_recv):
    owners, channels, width_x, width_y, width_z = sizes
    plane, lanes = width_x * width_y, SEG * STEP
    rows = pay_ref.shape[0]
    steps = rows // STEP
    groups = channels // PAIR
    gx, gy, gz = lax.axis_index("gx"), lax.axis_index("gy"), lax.axis_index("gz")
    mesh_id = pl.DeviceIdType.MESH

    barrier = pltpu.get_barrier_semaphore()
    for hop in range(1, owners):
        pl.semaphore_signal(barrier, inc=1, device_id={"gx": (gx + hop) % owners}, device_id_type=mesh_id)
    pl.semaphore_signal(barrier, inc=1, device_id={"gy": 1 - gy}, device_id_type=mesh_id)
    pl.semaphore_signal(barrier, inc=1, device_id={"gz": 1 - gz}, device_id_type=mesh_id)
    pl.semaphore_wait(barrier, owners + 1)

    sends = []
    for hop in range(1, owners):
        copy = pltpu.make_async_remote_copy(
            src_ref=pay_ref, dst_ref=arrived.at[hop - 1], send_sem=pay_send.at[hop - 1],
            recv_sem=pay_recv.at[hop - 1], device_id={"gx": (gx + hop) % owners}, device_id_type=mesh_id)
        copy.start()
        sends.append(copy)

    z_ids = lax.broadcasted_iota(jnp.int32, (width_z, lanes), 0).astype(jnp.float32)
    x_ids = (lax.broadcasted_iota(jnp.int32, (width_x, lanes), 0) + gx * width_x).astype(jnp.float32)
    y_ids = lax.broadcasted_iota(jnp.int32, (width_y, lanes), 0).astype(jnp.float32)

    def field(slot, step, which):
        return jnp.concatenate(
            [fields[slot, pl.ds(step * STEP + j, 1), which * SEG:(which + 1) * SEG] for j in range(STEP)],
            axis=1)

    def build(slot, step):
        away = field(slot, step, channels) - x_ids
        taps = jnp.exp(-(away * away) / (2.0 * spread_cells * spread_cells)) / TAP_SUM
        taps = jnp.where(jnp.abs(away) <= REACH, taps, 0.0).astype(jnp.bfloat16).astype(jnp.float32)
        hit = jnp.where(field(slot, step, channels + 1) == y_ids, 1.0, 0.0)
        for x in range(width_x):
            weights[slot * steps + step, x * width_y:(x + 1) * width_y, :] = (
                taps[x:x + 1, :] * hit).astype(jnp.bfloat16)

    def add(slot, step, group):
        here = field(slot, step, channels + 2) == z_ids
        spread = jnp.concatenate(
            [jnp.where(here, field(slot, step, group * PAIR + k), 0.0).astype(jnp.bfloat16)
             for k in range(PAIR)], axis=0)
        total[...] += lax.dot_general(
            weights[slot * steps + step], spread, (((1,), (1,)), ((), ())),
            preferred_element_type=jnp.float32)

    def deposit(first, last, group, building):
        def body(i, carry):
            slot, step = i // steps, i % steps
            if building:
                build(slot, step)
            add(slot, step, group)
            return carry

        lax.fori_loop(first * steps, last * steps, body, 0)

    def swap_z(group):
        x_buf[group] = total[...].astype(jnp.bfloat16)
        copy = pltpu.make_async_remote_copy(
            src_ref=x_buf.at[group], dst_ref=x_in.at[group], send_sem=zs_send.at[group],
            recv_sem=zs_recv.at[group], device_id={"gz": 1 - gz}, device_id_type=mesh_id)
        copy.start()
        return copy

    def filter_z(group, copy):
        copy.wait_recv()
        for k in range(PAIR):
            at = slice(k * width_z, (k + 1) * width_z)
            both = jnp.concatenate([x_buf[group, :, at], x_in[group, :, at]], axis=1)
            z_buf[group, :, at] = jnp.dot(
                both, wz_ref[...], preferred_element_type=jnp.float32).astype(jnp.bfloat16)
        sent = pltpu.make_async_remote_copy(
            src_ref=z_buf.at[group], dst_ref=z_in.at[group], send_sem=ys_send.at[group],
            recv_sem=ys_recv.at[group], device_id={"gy": 1 - gy}, device_id_type=mesh_id)
        sent.start()
        return sent

    block = wy_ref.shape[0]

    def filter_y(group, copy):
        copy.wait_recv()
        for b in range(plane // block):
            at = slice(b * block, (b + 1) * block)
            both = jnp.concatenate([z_buf[group, at, :], z_in[group, at, :]], axis=0)
            smooth = jnp.dot(wy_ref[...], both, preferred_element_type=jnp.float32)
            for k in range(PAIR):
                out_ref[group * PAIR + k, at, :] = (
                    fluid_ref[group * PAIR + k, at, :].astype(jnp.float32)
                    + smooth[:, k * width_z:(k + 1) * width_z]).astype(jnp.bfloat16)

    fields[0] = pay_ref[...].astype(jnp.float32)
    total[...] = jnp.zeros_like(total)
    for slot in range(owners):
        if slot:
            sends[slot - 1].wait_recv()
            fields[slot] = arrived[slot - 1].astype(jnp.float32)
        deposit(slot, slot + 1, 0, True)
    z_copies, y_copies = [swap_z(0)], []
    for group in range(1, groups):
        total[...] = jnp.zeros_like(total)
        deposit(0, 1, group, False)
        y_copies.append(filter_z(group - 1, z_copies[-1]))
        deposit(1, owners, group, False)
        z_copies.append(swap_z(group))
    y_copies.append(filter_z(groups - 1, z_copies[-1]))
    for group in range(groups):
        filter_y(group, y_copies[group])
    for copy in (*sends, *z_copies, *y_copies):
        copy.wait_send()


def on_device(parcel_values, parcel_owner, parcel_cell, live_counts, fluid_state):
    channels, count_dev = parcel_values.shape
    width_x, width_y, width_z = fluid_state.shape[1:]
    owners, plane, rows = lax.axis_size("gx"), width_x * width_y, count_dev // SEG
    is_live = jnp.arange(count_dev, dtype=jnp.int32) < live_counts[0]
    cell_x = jnp.where(is_live, parcel_owner[:, 0] * width_x + parcel_cell // (width_y * width_z), int(FAR))
    cell_y, cell_z = parcel_cell // width_z % width_y, parcel_cell % width_z
    payload = jnp.concatenate(
        [parcel_values[k].reshape(rows, SEG) for k in range(channels)]
        + [c.astype(jnp.bfloat16).reshape(rows, SEG) for c in (cell_x, cell_y, cell_z)], axis=1)
    own_y, other_y = periodic_pair(width_y)
    repeat = np.eye(256 // width_y, dtype=np.float32)
    weight_y = np.concatenate([np.kron(repeat, own_y), np.kron(repeat, other_y)], axis=1)
    own_z, other_z = periodic_pair(width_z)
    weight_z = np.concatenate([own_z.T, other_z.T], axis=0)
    sizes = (owners, channels, width_x, width_y, width_z)
    groups, wide = channels // PAIR, PAIR * width_z
    vmem = pl.BlockSpec(memory_space=pltpu.VMEM)
    coupled = pl.pallas_call(
        functools.partial(fused, sizes),
        out_shape=jax.ShapeDtypeStruct((channels, plane, width_z), jnp.bfloat16),
        in_specs=[vmem] * 4,
        out_specs=vmem,
        scratch_shapes=[
            pltpu.VMEM((owners - 1, rows, (channels + FIELDS) * SEG), jnp.bfloat16),
            pltpu.VMEM((owners, rows, (channels + FIELDS) * SEG), jnp.float32),
            pltpu.VMEM((owners * (rows // STEP), plane, SEG * STEP), jnp.bfloat16),
            pltpu.VMEM((plane, wide), jnp.float32),
            pltpu.VMEM((groups, plane, wide), jnp.bfloat16),
            pltpu.VMEM((groups, plane, wide), jnp.bfloat16),
            pltpu.VMEM((groups, plane, wide), jnp.bfloat16),
            pltpu.VMEM((groups, plane, wide), jnp.bfloat16),
            pltpu.SemaphoreType.DMA((owners - 1,)),
            pltpu.SemaphoreType.DMA((owners - 1,)),
            pltpu.SemaphoreType.DMA((groups,)),
            pltpu.SemaphoreType.DMA((groups,)),
            pltpu.SemaphoreType.DMA((groups,)),
            pltpu.SemaphoreType.DMA((groups,)),
        ],
        compiler_params=pltpu.CompilerParams(
            collective_id=0, has_side_effects=True, vmem_limit_bytes=48 << 20
        ),
    )(payload, fluid_state.reshape(channels, plane, width_z),
      jnp.asarray(weight_y, jnp.bfloat16), jnp.asarray(weight_z, jnp.bfloat16))
    return coupled.reshape(fluid_state.shape)


def solution(mesh):
    small = mesh.shape["gy"] == 2 and mesh.shape["gz"] == 2 and 2 <= mesh.shape["gx"] <= 4
    body = on_device if small else general
    in_specs = (
        P(None, ("grp", "gx", "gy", "gz")),
        P(("grp", "gx", "gy", "gz"), None),
        P(("grp", "gx", "gy", "gz")),
        P(("grp", "gx", "gy", "gz")),
        P(None, ("grp", "gx"), "gy", "gz"),
    )
    out_specs = P(None, ("grp", "gx"), "gy", "gz")
    return jax.shard_map(
        body, mesh=mesh, in_specs=in_specs, out_specs=out_specs, check_vma=False
    )
```

```python
import functools
import math

import jax
import jax.numpy as jnp
import numpy as np
from jax import lax
from jax.experimental import pallas as pl
from jax.experimental.pallas import tpu as pltpu
from jax.sharding import PartitionSpec as P

REACH = 16


spread_cells = 12.0


def padded(shard, sides, width):
    for axis, dim in sides:
        size, length = (lax.axis_size(axis), shard.shape[dim])
        up = [(i, (i + 1) % size) for i in range(size)]
        down = [(j, i) for i, j in up]
        last = lax.slice_in_dim(shard, length - width, length, axis=dim)
        initial = lax.slice_in_dim(shard, 0, width, axis=dim)
        before = lax.ppermute(last, axis, up)
        after = lax.ppermute(initial, axis, down)
        shard = jnp.concatenate([before, shard, after], axis=dim)
    return shard


def tap_curve(offsets):
    tap_grid = jnp.arange(2 * REACH + 1).astype(jnp.float32)
    tap_sum = jnp.sum(
        jnp.exp(-(tap_grid - REACH) * (tap_grid - REACH) / (2.0 * spread_cells * spread_cells))
    )
    return (
        jnp.exp(-(offsets - REACH) * (offsets - REACH) / (2.0 * spread_cells * spread_cells))
        / tap_sum
    )


def banded(out_rows, in_rows, shift):
    row_ids = lax.broadcasted_iota(jnp.int32, (out_rows, in_rows), 0)
    col_ids = lax.broadcasted_iota(jnp.int32, (out_rows, in_rows), 1)
    offset_ids = col_ids - row_ids + shift
    inside = (offset_ids >= 0) & (offset_ids <= 2 * REACH)
    values = tap_curve(offset_ids.astype(jnp.float32)).astype(jnp.bfloat16)
    return jnp.where(inside, values, jnp.zeros_like(values))


def running_sum(hits):
    shift = 1
    while shift < hits.shape[0]:
        hits = hits + jnp.pad(hits[:-shift], ((shift, 0), (0, 0)))
        shift *= 2
    return hits


def general(parcel_values, parcel_owner, parcel_cell, live_counts, fluid_state):
    channels, count_dev = parcel_values.shape
    width_x, width_y, width_z = (fluid_state.shape[1], fluid_state.shape[2], fluid_state.shape[3])
    owners = lax.axis_size("gx")
    capacity = 3 * count_dev // (2 * owners)
    owner_ids = parcel_owner[:, 0]
    local_rows = jnp.arange(count_dev, dtype=jnp.int32)
    is_live = local_rows < live_counts[0]
    owner_hits = (
        (owner_ids[:, None] == jnp.arange(owners, dtype=jnp.int32)[None, :]) & is_live[:, None]
    ).astype(jnp.int32)
    position = jnp.sum(running_sum(owner_hits) * owner_hits, axis=1) - 1
    slot_index = jnp.where(is_live, owner_ids * capacity + position, owners * capacity)
    cell_xpart = (parcel_cell // (width_y * width_z)).astype(jnp.bfloat16)
    cell_ypart = (parcel_cell // width_z % width_y).astype(jnp.bfloat16)
    cell_low = (parcel_cell % width_z).astype(jnp.bfloat16)
    send_rows = jnp.concatenate(
        [parcel_values, cell_xpart[None, :], cell_ypart[None, :], cell_low[None, :]], axis=0
    )
    packed = (
        jnp.zeros((channels + 3, owners * capacity), jnp.bfloat16)
        .at[:, slot_index]
        .set(send_rows, mode="drop")
    )
    packed = packed.reshape(channels + 3, owners, capacity)
    arrived = lax.all_to_all(packed, "gx", split_axis=1, concat_axis=1, tiled=True).reshape(
        channels + 3, owners * capacity
    )
    slot_total = owners * capacity
    block_rows = min(1024, slot_total)
    plane_cells = width_x * width_y
    high_grid = jnp.arange(plane_cells, dtype=jnp.float32)
    low_grid = jnp.arange(width_z, dtype=jnp.float32)

    def deposit(step_index, summed):
        window = lax.dynamic_slice_in_dim(arrived, step_index * block_rows, block_rows, 1)
        high_ids = window[channels].astype(jnp.float32) * width_y + window[channels + 1].astype(
            jnp.float32
        )
        high_hot = (high_ids[:, None] == high_grid[None, :]).astype(jnp.bfloat16)
        low_hot = (window[channels + 2].astype(jnp.float32)[:, None] == low_grid[None, :]).astype(
            jnp.bfloat16
        )
        weighted = window[:channels][:, :, None] * low_hot[None, :, :]
        return summed + jnp.einsum(
            "sh,csz->chz", high_hot, weighted, preferred_element_type=jnp.float32
        )

    summed = lax.fori_loop(
        0,
        slot_total // block_rows,
        deposit,
        jnp.zeros((channels, plane_cells, width_z), jnp.float32),
    )
    source = summed.reshape(channels, width_x, width_y, width_z).astype(jnp.bfloat16)
    flat_source = source.reshape(channels, width_x, width_y * width_z)
    pencil = lax.all_to_all(flat_source, "gx", split_axis=2, concat_axis=1, tiled=True)
    full_x = pencil.shape[1]
    smoothed = jnp.einsum(
        "ij,cjk->cik", banded(full_x, full_x, REACH), pencil, preferred_element_type=jnp.float32
    ).astype(jnp.bfloat16)
    after_x = lax.all_to_all(smoothed, "gx", split_axis=1, concat_axis=2, tiled=True)
    after_x = after_x.reshape(channels, width_x, width_y, width_z)
    extended_y = padded(after_x, (("gy", 2),), REACH)
    after_y = jnp.einsum(
        "ij,cxjz->cxiz",
        banded(width_y, width_y + 2 * REACH, 0),
        extended_y,
        preferred_element_type=jnp.float32,
    ).astype(jnp.bfloat16)
    extended_z = padded(after_y, (("gz", 3),), REACH)
    smooth_z = jnp.einsum(
        "cxyj,ij->cxyi",
        extended_z,
        banded(width_z, width_z + 2 * REACH, 0),
        preferred_element_type=jnp.float32,
    )
    return (fluid_state.astype(jnp.float32) + smooth_z).astype(jnp.bfloat16)


SEG = 256
STEP = 4
FIELDS = 3
PAIR = 2
FAR = 1024.0
TAP_SUM = float(
    sum(math.exp(-((t - REACH) ** 2) / (2.0 * spread_cells**2)) for t in range(2 * REACH + 1))
)


def tap_matrix(offsets):
    values = np.exp(-((offsets - REACH) ** 2) / (2.0 * spread_cells**2)) / TAP_SUM
    values = values.astype(np.float32).astype(jnp.bfloat16).astype(np.float32)
    return np.where((offsets >= 0) & (offsets <= 2 * REACH), values, 0.0)


def periodic_pair(width):
    out_at, in_at = np.arange(width)[:, None], np.arange(width)[None, :]
    own = tap_matrix(in_at - out_at + REACH)
    other = tap_matrix(in_at - width - out_at + REACH) + tap_matrix(in_at + width - out_at + REACH)
    return own, other


def log2(size):
    return size.bit_length() - 1


def fused(sizes, values_hbm, owner_hbm, cell_hbm, live_ref, fluid_hbm, wy_hbm, wz_hbm, out_ref,
          values_ref, owner_ref, cell_ref, payload, arrived, fields, plain, weights, total, fluid, wy, wz, one, one_in, two, two_in,
          load_sem, pay_send, pay_recv, one_send, one_recv, two_send, two_recv):
    owners, channels, width_x, width_y, width_z = sizes
    plane, lanes = width_x * width_y, SEG * STEP
    rows = payload.shape[0]
    steps = rows // STEP
    groups = channels // PAIR
    gx, gy, gz = lax.axis_index("gx"), lax.axis_index("gy"), lax.axis_index("gz")
    mesh_id = pl.DeviceIdType.MESH

    loads = []
    pairs = ((values_hbm, values_ref), (owner_hbm, owner_ref), (cell_hbm, cell_ref),
             (fluid_hbm, fluid), (wy_hbm, wy), (wz_hbm, wz))
    for at, (source, dest) in enumerate(pairs):
        copy = pltpu.make_async_copy(source, dest, load_sem.at[at])
        copy.start()
        loads.append(copy)

    barrier = pltpu.get_barrier_semaphore()
    for hop in range(1, owners):
        pl.semaphore_signal(barrier, inc=1, device_id={"gx": (gx + hop) % owners}, device_id_type=mesh_id)
    pl.semaphore_signal(barrier, inc=1, device_id={"gy": 1 - gy}, device_id_type=mesh_id)
    pl.semaphore_signal(barrier, inc=1, device_id={"gz": 1 - gz}, device_id_type=mesh_id)

    for copy in loads[:3]:
        copy.wait()
    width = cell_ref.shape[1]
    row_ids = lax.broadcasted_iota(jnp.int32, cell_ref.shape, 0) * width
    is_live = row_ids + lax.broadcasted_iota(jnp.int32, cell_ref.shape, 1) < live_ref[0]
    cell = cell_ref[...]
    cell_x = owner_ref[...] * width_x + lax.shift_right_logical(cell, log2(width_y * width_z))
    cells = (
        jnp.where(is_live, cell_x.astype(jnp.float32), FAR),
        (lax.shift_right_logical(cell, log2(width_z)) & (width_y - 1)).astype(jnp.float32),
        (cell & (width_z - 1)).astype(jnp.float32),
    )
    plain[...] = values_ref[...].astype(jnp.float32)
    for row in range(rows):
        for k in range(channels):
            fields[0, row:row + 1, k * SEG:(k + 1) * SEG] = plain[k:k + 1, row * SEG:(row + 1) * SEG]
        for k, part in enumerate(cells):
            for j in range(SEG // width):
                start, line = (channels + k) * SEG + j * width, row * (SEG // width) + j
                fields[0, row:row + 1, start:start + width] = part[line:line + 1, :]
    payload[...] = fields[0].astype(jnp.bfloat16)
    pl.semaphore_wait(barrier, owners + 1)

    sends = []
    for hop in range(1, owners):
        copy = pltpu.make_async_remote_copy(
            src_ref=payload, dst_ref=arrived.at[hop - 1], send_sem=pay_send.at[hop - 1],
            recv_sem=pay_recv.at[hop - 1], device_id={"gx": (gx + hop) % owners}, device_id_type=mesh_id)
        copy.start()
        sends.append(copy)

    z_ids = lax.broadcasted_iota(jnp.int32, (width_z, lanes), 0).astype(jnp.float32)
    x_ids = (lax.broadcasted_iota(jnp.int32, (width_x, lanes), 0) + gx * width_x).astype(jnp.float32)
    y_ids = lax.broadcasted_iota(jnp.int32, (width_y, lanes), 0).astype(jnp.float32)

    def field(slot, step, which):
        return jnp.concatenate(
            [fields[slot, pl.ds(step * STEP + j, 1), which * SEG:(which + 1) * SEG] for j in range(STEP)],
            axis=1)

    def build(slot, step):
        away = field(slot, step, channels) - x_ids
        taps = jnp.exp(-(away * away) / (2.0 * spread_cells * spread_cells)) / TAP_SUM
        taps = jnp.where(jnp.abs(away) <= REACH, taps, 0.0).astype(jnp.bfloat16).astype(jnp.float32)
        hit = jnp.where(field(slot, step, channels + 1) == y_ids, 1.0, 0.0)
        for x in range(width_x):
            weights[slot * steps + step, x * width_y:(x + 1) * width_y, :] = (
                taps[x:x + 1, :] * hit).astype(jnp.bfloat16)

    def add(slot, step, group):
        here = field(slot, step, channels + 2) == z_ids
        spread = jnp.concatenate(
            [jnp.where(here, field(slot, step, group * PAIR + k), 0.0).astype(jnp.bfloat16)
             for k in range(PAIR)], axis=0)
        total[group] += lax.dot_general(
            weights[slot * steps + step], spread, (((1,), (1,)), ((), ())),
            preferred_element_type=jnp.float32)

    def deposit(first, last, group, building):
        def body(i, carry):
            slot, step = i // steps, i % steps
            if building:
                build(slot, step)
            add(slot, step, group)
            return carry

        lax.fori_loop(first * steps, last * steps, body, 0, unroll=steps)

    def swap(group, axis, buffer, landing, sent, received):
        me = gy if axis == "gy" else gz
        copy = pltpu.make_async_remote_copy(
            src_ref=buffer.at[group], dst_ref=landing.at[group], send_sem=sent.at[group],
            recv_sem=received.at[group], device_id={axis: 1 - me}, device_id_type=mesh_id)
        copy.start()
        return copy

    def begin(group, axis):
        one[group] = total[group].astype(jnp.bfloat16)
        return swap(group, axis, one, one_in, one_send, one_recv)

    block = wy_hbm.shape[0]
    column = [slice(k * width_z, (k + 1) * width_z) for k in range(PAIR)]
    spans = [slice(b * block, (b + 1) * block) for b in range(plane // block)]

    def along_z(own, other, group, k):
        both = jnp.concatenate([own[group, :, column[k]], other[group, :, column[k]]], axis=1)
        return jnp.dot(both, wz[...], preferred_element_type=jnp.float32)

    def along_y(own, other, group, span):
        both = jnp.concatenate([own[group, span, :], other[group, span, :]], axis=0)
        return jnp.dot(wy[...], both, preferred_element_type=jnp.float32)

    def z_then_send_y(group, copy):
        copy.wait_recv()
        for k in range(PAIR):
            two[group, :, column[k]] = along_z(one, one_in, group, k).astype(jnp.bfloat16)
        return swap(group, "gy", two, two_in, two_send, two_recv)

    def y_then_send_z(group, copy):
        copy.wait_recv()
        for span in spans:
            two[group, span, :] = along_y(one, one_in, group, span).astype(jnp.bfloat16)
        return swap(group, "gz", two, two_in, two_send, two_recv)

    def end_with_z(group, copy):
        copy.wait_recv()
        for k in range(PAIR):
            out_ref[group * PAIR + k] = (
                fluid[group * PAIR + k].astype(jnp.float32) + along_z(two, two_in, group, k)
            ).astype(jnp.bfloat16)

    def end_with_y(group, copy):
        copy.wait_recv()
        for span in spans:
            smooth = along_y(two, two_in, group, span)
            for k in range(PAIR):
                out_ref[group * PAIR + k, span, :] = (
                    fluid[group * PAIR + k, span, :].astype(jnp.float32) + smooth[:, column[k]]
                ).astype(jnp.bfloat16)

    total[...] = jnp.zeros_like(total)
    for group in range(groups):
        deposit(0, 1, group, group == 0)
    for slot in range(1, owners):
        sends[slot - 1].wait_recv()
        fields[slot] = arrived[slot - 1].astype(jnp.float32)
        deposit(slot, slot + 1, 0, True)
    firsts, seconds = [begin(0, "gy")], [None]
    for copy in loads[3:]:
        copy.wait()
    for group in range(1, groups):
        deposit(1, 2, group, False)
        if group > 1:
            seconds.append(z_then_send_y(group - 1, firsts[-1]))
        deposit(2, owners, group, False)
        firsts.append(begin(group, "gz"))
    seconds.append(z_then_send_y(groups - 1, firsts[-1]))
    seconds[0] = y_then_send_z(0, firsts[0])
    end_with_z(0, seconds[0])
    for group in range(1, groups):
        end_with_y(group, seconds[group])
    for copy in (*sends, *firsts, *seconds):
        copy.wait_send()


def on_device(parcel_values, parcel_owner, parcel_cell, live_counts, fluid_state):
    channels, count_dev = parcel_values.shape
    width_x, width_y, width_z = fluid_state.shape[1:]
    owners, plane, rows = lax.axis_size("gx"), width_x * width_y, count_dev // SEG
    own_y, other_y = periodic_pair(width_y)
    repeat = np.eye(256 // width_y, dtype=np.float32)
    weight_y = np.concatenate([np.kron(repeat, own_y), np.kron(repeat, other_y)], axis=1)
    own_z, other_z = periodic_pair(width_z)
    weight_z = np.concatenate([own_z.T, other_z.T], axis=0)
    sizes = (owners, channels, width_x, width_y, width_z)
    groups, wide = channels // PAIR, PAIR * width_z
    vmem, hbm = pl.BlockSpec(memory_space=pltpu.VMEM), pl.BlockSpec(memory_space=pltpu.HBM)
    lines = (count_dev // 128, 128)
    coupled = pl.pallas_call(
        functools.partial(fused, sizes),
        out_shape=jax.ShapeDtypeStruct((channels, plane, width_z), jnp.bfloat16),
        in_specs=[hbm] * 3 + [pl.BlockSpec(memory_space=pltpu.SMEM)] + [hbm] * 3,
        out_specs=vmem,
        scratch_shapes=[
            pltpu.VMEM((channels, count_dev), jnp.bfloat16),
            pltpu.VMEM(lines, jnp.int32),
            pltpu.VMEM(lines, jnp.int32),
            pltpu.VMEM((rows, (channels + FIELDS) * SEG), jnp.bfloat16),
            pltpu.VMEM((owners - 1, rows, (channels + FIELDS) * SEG), jnp.bfloat16),
            pltpu.VMEM((owners, rows, (channels + FIELDS) * SEG), jnp.float32),
            pltpu.VMEM((channels, count_dev), jnp.float32),
            pltpu.VMEM((owners * (rows // STEP), plane, SEG * STEP), jnp.bfloat16),
            pltpu.VMEM((groups, plane, wide), jnp.float32),
            pltpu.VMEM((channels, plane, width_z), jnp.bfloat16),
            pltpu.VMEM(weight_y.shape, jnp.bfloat16),
            pltpu.VMEM(weight_z.shape, jnp.bfloat16),
            pltpu.VMEM((groups, plane, wide), jnp.bfloat16),
            pltpu.VMEM((groups, plane, wide), jnp.bfloat16),
            pltpu.VMEM((groups, plane, wide), jnp.bfloat16),
            pltpu.VMEM((groups, plane, wide), jnp.bfloat16),
            pltpu.SemaphoreType.DMA((6,)),
            pltpu.SemaphoreType.DMA((owners - 1,)),
            pltpu.SemaphoreType.DMA((owners - 1,)),
            pltpu.SemaphoreType.DMA((groups,)),
            pltpu.SemaphoreType.DMA((groups,)),
            pltpu.SemaphoreType.DMA((groups,)),
            pltpu.SemaphoreType.DMA((groups,)),
        ],
        compiler_params=pltpu.CompilerParams(
            collective_id=0, has_side_effects=True, vmem_limit_bytes=63 << 20
        ),
    )(parcel_values, parcel_owner.reshape(lines), parcel_cell.reshape(lines), live_counts,
      fluid_state.reshape(channels, plane, width_z),
      jnp.asarray(weight_y, jnp.bfloat16), jnp.asarray(weight_z, jnp.bfloat16))
    return coupled.reshape(fluid_state.shape)


def solution(mesh):
    small = mesh.shape["gy"] == 2 and mesh.shape["gz"] == 2 and 3 <= mesh.shape["gx"] <= 4
    body = on_device if small else general
    in_specs = (
        P(None, ("grp", "gx", "gy", "gz")),
        P(("grp", "gx", "gy", "gz"), None),
        P(("grp", "gx", "gy", "gz")),
        P(("grp", "gx", "gy", "gz")),
        P(None, ("grp", "gx"), "gy", "gz"),
    )
    out_specs = P(None, ("grp", "gx"), "gy", "gz")
    return jax.shard_map(
        body, mesh=mesh, in_specs=in_specs, out_specs=out_specs, check_vma=False
    )
```

```python
import functools
import math

import jax
import jax.numpy as jnp
import numpy as np
from jax import lax
from jax.experimental import pallas as pl
from jax.experimental.pallas import tpu as pltpu
from jax.sharding import PartitionSpec as P

REACH = 16


spread_cells = 12.0


def padded(shard, sides, width):
    for axis, dim in sides:
        size, length = (lax.axis_size(axis), shard.shape[dim])
        up = [(i, (i + 1) % size) for i in range(size)]
        down = [(j, i) for i, j in up]
        last = lax.slice_in_dim(shard, length - width, length, axis=dim)
        initial = lax.slice_in_dim(shard, 0, width, axis=dim)
        before = lax.ppermute(last, axis, up)
        after = lax.ppermute(initial, axis, down)
        shard = jnp.concatenate([before, shard, after], axis=dim)
    return shard


def tap_curve(offsets):
    tap_grid = jnp.arange(2 * REACH + 1).astype(jnp.float32)
    tap_sum = jnp.sum(
        jnp.exp(-(tap_grid - REACH) * (tap_grid - REACH) / (2.0 * spread_cells * spread_cells))
    )
    return (
        jnp.exp(-(offsets - REACH) * (offsets - REACH) / (2.0 * spread_cells * spread_cells))
        / tap_sum
    )


def banded(out_rows, in_rows, shift):
    row_ids = lax.broadcasted_iota(jnp.int32, (out_rows, in_rows), 0)
    col_ids = lax.broadcasted_iota(jnp.int32, (out_rows, in_rows), 1)
    offset_ids = col_ids - row_ids + shift
    inside = (offset_ids >= 0) & (offset_ids <= 2 * REACH)
    values = tap_curve(offset_ids.astype(jnp.float32)).astype(jnp.bfloat16)
    return jnp.where(inside, values, jnp.zeros_like(values))


def running_sum(hits):
    shift = 1
    while shift < hits.shape[0]:
        hits = hits + jnp.pad(hits[:-shift], ((shift, 0), (0, 0)))
        shift *= 2
    return hits


def general(parcel_values, parcel_owner, parcel_cell, live_counts, fluid_state):
    channels, count_dev = parcel_values.shape
    width_x, width_y, width_z = (fluid_state.shape[1], fluid_state.shape[2], fluid_state.shape[3])
    owners = lax.axis_size("gx")
    capacity = 3 * count_dev // (2 * owners)
    owner_ids = parcel_owner[:, 0]
    local_rows = jnp.arange(count_dev, dtype=jnp.int32)
    is_live = local_rows < live_counts[0]
    owner_hits = (
        (owner_ids[:, None] == jnp.arange(owners, dtype=jnp.int32)[None, :]) & is_live[:, None]
    ).astype(jnp.int32)
    position = jnp.sum(running_sum(owner_hits) * owner_hits, axis=1) - 1
    slot_index = jnp.where(is_live, owner_ids * capacity + position, owners * capacity)
    cell_xpart = (parcel_cell // (width_y * width_z)).astype(jnp.bfloat16)
    cell_ypart = (parcel_cell // width_z % width_y).astype(jnp.bfloat16)
    cell_low = (parcel_cell % width_z).astype(jnp.bfloat16)
    send_rows = jnp.concatenate(
        [parcel_values, cell_xpart[None, :], cell_ypart[None, :], cell_low[None, :]], axis=0
    )
    packed = (
        jnp.zeros((channels + 3, owners * capacity), jnp.bfloat16)
        .at[:, slot_index]
        .set(send_rows, mode="drop")
    )
    packed = packed.reshape(channels + 3, owners, capacity)
    arrived = lax.all_to_all(packed, "gx", split_axis=1, concat_axis=1, tiled=True).reshape(
        channels + 3, owners * capacity
    )
    slot_total = owners * capacity
    block_rows = min(1024, slot_total)
    plane_cells = width_x * width_y
    high_grid = jnp.arange(plane_cells, dtype=jnp.float32)
    low_grid = jnp.arange(width_z, dtype=jnp.float32)

    def deposit(step_index, summed):
        window = lax.dynamic_slice_in_dim(arrived, step_index * block_rows, block_rows, 1)
        high_ids = window[channels].astype(jnp.float32) * width_y + window[channels + 1].astype(
            jnp.float32
        )
        high_hot = (high_ids[:, None] == high_grid[None, :]).astype(jnp.bfloat16)
        low_hot = (window[channels + 2].astype(jnp.float32)[:, None] == low_grid[None, :]).astype(
            jnp.bfloat16
        )
        weighted = window[:channels][:, :, None] * low_hot[None, :, :]
        return summed + jnp.einsum(
            "sh,csz->chz", high_hot, weighted, preferred_element_type=jnp.float32
        )

    summed = lax.fori_loop(
        0,
        slot_total // block_rows,
        deposit,
        jnp.zeros((channels, plane_cells, width_z), jnp.float32),
    )
    source = summed.reshape(channels, width_x, width_y, width_z).astype(jnp.bfloat16)
    flat_source = source.reshape(channels, width_x, width_y * width_z)
    pencil = lax.all_to_all(flat_source, "gx", split_axis=2, concat_axis=1, tiled=True)
    full_x = pencil.shape[1]
    smoothed = jnp.einsum(
        "ij,cjk->cik", banded(full_x, full_x, REACH), pencil, preferred_element_type=jnp.float32
    ).astype(jnp.bfloat16)
    after_x = lax.all_to_all(smoothed, "gx", split_axis=1, concat_axis=2, tiled=True)
    after_x = after_x.reshape(channels, width_x, width_y, width_z)
    extended_y = padded(after_x, (("gy", 2),), REACH)
    after_y = jnp.einsum(
        "ij,cxjz->cxiz",
        banded(width_y, width_y + 2 * REACH, 0),
        extended_y,
        preferred_element_type=jnp.float32,
    ).astype(jnp.bfloat16)
    extended_z = padded(after_y, (("gz", 3),), REACH)
    smooth_z = jnp.einsum(
        "cxyj,ij->cxyi",
        extended_z,
        banded(width_z, width_z + 2 * REACH, 0),
        preferred_element_type=jnp.float32,
    )
    return (fluid_state.astype(jnp.float32) + smooth_z).astype(jnp.bfloat16)


SEG = 256
STEP = 4
FIELDS = 3
PAIR = 2
FAR = 1024.0
TAP_SUM = float(
    sum(math.exp(-((t - REACH) ** 2) / (2.0 * spread_cells**2)) for t in range(2 * REACH + 1))
)


def tap_matrix(offsets):
    values = np.exp(-((offsets - REACH) ** 2) / (2.0 * spread_cells**2)) / TAP_SUM
    values = values.astype(np.float32).astype(jnp.bfloat16).astype(np.float32)
    return np.where((offsets >= 0) & (offsets <= 2 * REACH), values, 0.0)


def periodic_pair(width):
    out_at, in_at = np.arange(width)[:, None], np.arange(width)[None, :]
    own = tap_matrix(in_at - out_at + REACH)
    other = tap_matrix(in_at - width - out_at + REACH) + tap_matrix(in_at + width - out_at + REACH)
    return own, other


def log2(size):
    return size.bit_length() - 1


def fused(sizes, values_hbm, owner_hbm, cell_hbm, live_ref, fluid_hbm, wy_hbm, wz_hbm, out_ref,
          values_ref, owner_ref, cell_ref, payload, arrived, fields, plain, weights, total, fluid, wy, wz, one, one_in, two, two_in,
          load_sem, pay_send, pay_recv, one_send, one_recv, two_send, two_recv):
    owners, channels, width_x, width_y, width_z = sizes
    plane, lanes = width_x * width_y, SEG * STEP
    rows = payload.shape[0]
    steps = rows // STEP
    groups = channels // PAIR
    gx, gy, gz = lax.axis_index("gx"), lax.axis_index("gy"), lax.axis_index("gz")
    mesh_id = pl.DeviceIdType.MESH

    loads = []
    pairs = ((values_hbm, values_ref), (owner_hbm, owner_ref), (cell_hbm, cell_ref),
             (fluid_hbm, fluid), (wy_hbm, wy), (wz_hbm, wz))
    for at, (source, dest) in enumerate(pairs):
        copy = pltpu.make_async_copy(source, dest, load_sem.at[at])
        copy.start()
        loads.append(copy)

    barrier = pltpu.get_barrier_semaphore()
    for hop in range(1, owners):
        pl.semaphore_signal(barrier, inc=1, device_id={"gx": (gx + hop) % owners}, device_id_type=mesh_id)
    pl.semaphore_signal(barrier, inc=1, device_id={"gy": 1 - gy}, device_id_type=mesh_id)
    pl.semaphore_signal(barrier, inc=1, device_id={"gz": 1 - gz}, device_id_type=mesh_id)

    for copy in loads[:3]:
        copy.wait()
    width = cell_ref.shape[1]
    row_ids = lax.broadcasted_iota(jnp.int32, cell_ref.shape, 0) * width
    is_live = row_ids + lax.broadcasted_iota(jnp.int32, cell_ref.shape, 1) < live_ref[0]
    cell = cell_ref[...]
    cell_x = owner_ref[...] * width_x + lax.shift_right_logical(cell, log2(width_y * width_z))
    cells = (
        jnp.where(is_live, cell_x.astype(jnp.float32), FAR),
        (lax.shift_right_logical(cell, log2(width_z)) & (width_y - 1)).astype(jnp.float32),
        (cell & (width_z - 1)).astype(jnp.float32),
    )
    plain[...] = values_ref[...].astype(jnp.float32)
    for row in range(rows):
        for k in range(channels):
            fields[0, row:row + 1, k * SEG:(k + 1) * SEG] = plain[k:k + 1, row * SEG:(row + 1) * SEG]
        for k, part in enumerate(cells):
            for j in range(SEG // width):
                start, line = (channels + k) * SEG + j * width, row * (SEG // width) + j
                fields[0, row:row + 1, start:start + width] = part[line:line + 1, :]
    payload[...] = fields[0].astype(jnp.bfloat16)
    pl.semaphore_wait(barrier, owners + 1)

    sends = []
    for hop in range(1, owners):
        copy = pltpu.make_async_remote_copy(
            src_ref=payload, dst_ref=arrived.at[hop - 1], send_sem=pay_send.at[hop - 1],
            recv_sem=pay_recv.at[hop - 1], device_id={"gx": (gx + hop) % owners}, device_id_type=mesh_id)
        copy.start()
        sends.append(copy)

    z_ids = lax.broadcasted_iota(jnp.int32, (width_z, lanes), 0).astype(jnp.float32)
    x_ids = (lax.broadcasted_iota(jnp.int32, (width_x, lanes), 0) + gx * width_x).astype(jnp.float32)
    y_ids = lax.broadcasted_iota(jnp.int32, (width_y, lanes), 0).astype(jnp.float32)

    def field(slot, step, which):
        return jnp.concatenate(
            [fields[slot, pl.ds(step * STEP + j, 1), pl.ds(pl.multiple_of(which * SEG, SEG), SEG)]
             for j in range(STEP)],
            axis=1)

    def build(slot, step):
        away = field(slot, step, channels) - x_ids
        taps = jnp.exp(-(away * away) / (2.0 * spread_cells * spread_cells)) / TAP_SUM
        taps = jnp.where(jnp.abs(away) <= REACH, taps, 0.0).astype(jnp.bfloat16).astype(jnp.float32)
        hit = jnp.where(field(slot, step, channels + 1) == y_ids, 1.0, 0.0)
        for x in range(width_x):
            weights[slot * steps + step, x * width_y:(x + 1) * width_y, :] = (
                taps[x:x + 1, :] * hit).astype(jnp.bfloat16)

    def add(slot, step, group):
        here = field(slot, step, channels + 2) == z_ids
        spread = jnp.concatenate(
            [jnp.where(here, field(slot, step, group * PAIR + k), 0.0).astype(jnp.bfloat16)
             for k in range(PAIR)], axis=0)
        total[group] += lax.dot_general(
            weights[slot * steps + step], spread, (((1,), (1,)), ((), ())),
            preferred_element_type=jnp.float32)

    def build_slot(slot):
        def body(step, carry):
            build(slot, step)
            return carry

        lax.fori_loop(0, steps, body, 0)

    def add_slot(slot, group):
        for step in range(steps):
            add(slot, step, group)

    def swap(group, axis, buffer, landing, sent, received):
        me = gy if axis == "gy" else gz
        return pltpu.make_async_remote_copy(
            src_ref=buffer.at[group], dst_ref=landing.at[group], send_sem=sent.at[group],
            recv_sem=received.at[group], device_id={axis: 1 - me}, device_id_type=mesh_id)

    firsts = [swap(g, "gz" if g else "gy", one, one_in, one_send, one_recv) for g in range(groups)]
    seconds = [swap(g, "gy" if g else "gz", two, two_in, two_send, two_recv) for g in range(groups)]

    def begin(group):
        one[group] = total[group].astype(jnp.bfloat16)
        firsts[group].start()

    block = wy_hbm.shape[0]
    column = [slice(k * width_z, (k + 1) * width_z) for k in range(PAIR)]
    spans = [slice(b * block, (b + 1) * block) for b in range(plane // block)]

    def along_z(own, other, group, k):
        both = jnp.concatenate([own[group, :, column[k]], other[group, :, column[k]]], axis=1)
        return jnp.dot(both, wz[...], preferred_element_type=jnp.float32)

    def along_y(own, other, group, span):
        both = jnp.concatenate([own[group, span, :], other[group, span, :]], axis=0)
        return jnp.dot(wy[...], both, preferred_element_type=jnp.float32)

    def z_then_send_y(group):
        firsts[group].wait_recv()
        for k in range(PAIR):
            two[group, :, column[k]] = along_z(one, one_in, group, k).astype(jnp.bfloat16)
        seconds[group].start()

    def y_then_send_z(group):
        firsts[group].wait_recv()
        for span in spans:
            two[group, span, :] = along_y(one, one_in, group, span).astype(jnp.bfloat16)
        seconds[group].start()

    def end_with_z(group, copy):
        copy.wait_recv()
        for k in range(PAIR):
            out_ref[group * PAIR + k] = (
                fluid[group * PAIR + k].astype(jnp.float32) + along_z(two, two_in, group, k)
            ).astype(jnp.bfloat16)

    def end_with_y(group, copy):
        copy.wait_recv()
        for span in spans:
            smooth = along_y(two, two_in, group, span)
            for k in range(PAIR):
                out_ref[group * PAIR + k, span, :] = (
                    fluid[group * PAIR + k, span, :].astype(jnp.float32) + smooth[:, column[k]]
                ).astype(jnp.bfloat16)

    total[...] = jnp.zeros_like(total)
    build_slot(0)

    def own(group, carry):
        add_slot(0, group)
        return carry

    lax.fori_loop(0, groups, own, 0)
    for copy in loads[3:]:
        copy.wait()

    def turn(t, carry):
        slot, group = lax.rem(t, owners - 1) + 1, lax.div(t, owners - 1)

        @pl.when(t < owners - 1)
        def _():
            pltpu.make_async_remote_copy(
                src_ref=payload, dst_ref=arrived.at[slot - 1], send_sem=pay_send.at[slot - 1],
                recv_sem=pay_recv.at[slot - 1],
                device_id={"gx": (gx + slot) % owners}, device_id_type=mesh_id).wait_recv()
            fields[slot] = arrived[slot - 1].astype(jnp.float32)
            build_slot(slot)

        add_slot(slot, group)
        for g in range(groups - 1):
            @pl.when(t == (g + 1) * (owners - 1) - 1)
            def _(g=g):
                begin(g)

            if g:
                @pl.when(t == (g + 1) * (owners - 1))
                def _(g=g):
                    z_then_send_y(g)

        return carry

    lax.fori_loop(0, groups * (owners - 1), turn, 0)
    begin(groups - 1)
    z_then_send_y(groups - 1)
    y_then_send_z(0)
    end_with_z(0, seconds[0])
    for group in range(1, groups):
        end_with_y(group, seconds[group])
    for copy in (*sends, *firsts, *seconds):
        copy.wait_send()


def on_device(parcel_values, parcel_owner, parcel_cell, live_counts, fluid_state):
    channels, count_dev = parcel_values.shape
    width_x, width_y, width_z = fluid_state.shape[1:]
    owners, plane, rows = lax.axis_size("gx"), width_x * width_y, count_dev // SEG
    own_y, other_y = periodic_pair(width_y)
    repeat = np.eye(256 // width_y, dtype=np.float32)
    weight_y = np.concatenate([np.kron(repeat, own_y), np.kron(repeat, other_y)], axis=1)
    own_z, other_z = periodic_pair(width_z)
    weight_z = np.concatenate([own_z.T, other_z.T], axis=0)
    sizes = (owners, channels, width_x, width_y, width_z)
    groups, wide = channels // PAIR, PAIR * width_z
    vmem, hbm = pl.BlockSpec(memory_space=pltpu.VMEM), pl.BlockSpec(memory_space=pltpu.HBM)
    lines = (count_dev // 128, 128)
    coupled = pl.pallas_call(
        functools.partial(fused, sizes),
        out_shape=jax.ShapeDtypeStruct((channels, plane, width_z), jnp.bfloat16),
        in_specs=[hbm] * 3 + [pl.BlockSpec(memory_space=pltpu.SMEM)] + [hbm] * 3,
        out_specs=vmem,
        scratch_shapes=[
            pltpu.VMEM((channels, count_dev), jnp.bfloat16),
            pltpu.VMEM(lines, jnp.int32),
            pltpu.VMEM(lines, jnp.int32),
            pltpu.VMEM((rows, (channels + FIELDS) * SEG), jnp.bfloat16),
            pltpu.VMEM((owners - 1, rows, (channels + FIELDS) * SEG), jnp.bfloat16),
            pltpu.VMEM((owners, rows, (channels + FIELDS) * SEG), jnp.float32),
            pltpu.VMEM((channels, count_dev), jnp.float32),
            pltpu.VMEM((owners * (rows // STEP), plane, SEG * STEP), jnp.bfloat16),
            pltpu.VMEM((groups, plane, wide), jnp.float32),
            pltpu.VMEM((channels, plane, width_z), jnp.bfloat16),
            pltpu.VMEM(weight_y.shape, jnp.bfloat16),
            pltpu.VMEM(weight_z.shape, jnp.bfloat16),
            pltpu.VMEM((groups, plane, wide), jnp.bfloat16),
            pltpu.VMEM((groups, plane, wide), jnp.bfloat16),
            pltpu.VMEM((groups, plane, wide), jnp.bfloat16),
            pltpu.VMEM((groups, plane, wide), jnp.bfloat16),
            pltpu.SemaphoreType.DMA((6,)),
            pltpu.SemaphoreType.DMA((owners - 1,)),
            pltpu.SemaphoreType.DMA((owners - 1,)),
            pltpu.SemaphoreType.DMA((groups,)),
            pltpu.SemaphoreType.DMA((groups,)),
            pltpu.SemaphoreType.DMA((groups,)),
            pltpu.SemaphoreType.DMA((groups,)),
        ],
        compiler_params=pltpu.CompilerParams(
            collective_id=0, has_side_effects=True, vmem_limit_bytes=63 << 20
        ),
    )(parcel_values, parcel_owner.reshape(lines), parcel_cell.reshape(lines), live_counts,
      fluid_state.reshape(channels, plane, width_z),
      jnp.asarray(weight_y, jnp.bfloat16), jnp.asarray(weight_z, jnp.bfloat16))
    return coupled.reshape(fluid_state.shape)


def solution(mesh):
    small = mesh.shape["gy"] == 2 and mesh.shape["gz"] == 2 and 3 <= mesh.shape["gx"] <= 4
    body = on_device if small else general
    in_specs = (
        P(None, ("grp", "gx", "gy", "gz")),
        P(("grp", "gx", "gy", "gz"), None),
        P(("grp", "gx", "gy", "gz")),
        P(("grp", "gx", "gy", "gz")),
        P(None, ("grp", "gx"), "gy", "gz"),
    )
    out_specs = P(None, ("grp", "gx"), "gy", "gz")
    return jax.shard_map(
        body, mesh=mesh, in_specs=in_specs, out_specs=out_specs, check_vma=False
    )
```
